32 devices in a mesh: row: 4 (over y, core), col: 8 (over z, x).
Axes of the slice: x: 2, y: 2, z: 4, core: 2. Of those that a mesh axis runs over, the one named last changes fastest.
Arguments:
- grad_out: bfloat16 [1024, 16384], P('col', 'row'), may hold values from -0.1875 to 0.1875
- activations: bfloat16 [1024, 16384], P('row', 'col'), may hold values from -6 to 6
- projector: bfloat16 [16384, 1024], P('row'), may hold values from -0.046875 to 0.046875
- weight: float32 [16384, 16384], P('row', 'col'), may hold values from -6 to 6
- first_moment: float32 [1024, 16384], P('row', 'col'), may hold values from -3 to 3
- second_moment: float32 [1024, 16384], P('row', 'col'), may hold values from 0.25 to 4
Outputs:
- new_weight: float32 [16384, 16384], P('row', 'col')
- new_first: float32 [1024, 16384], P('row', 'col')
- new_second: float32 [1024, 16384], P('row', 'col')
The draws below stay inside these ranges and needn't reach their ends.
All inputs are finite; a program needn't handle non-finite values.
Results may differ from the reference program's by a relative error of at most 0.0015.
Values may be sent and summed in bfloat16 or wider, within the bound.
No kernel may reach another device: no remote copies, remote signals or barrier semaphores. Data moves between devices by JAX's collectives and lax.ppermute only.
A program may use at most 192 MiB of HBM per device.

```python
import math
import jax
import jax.numpy as jnp
from jax import lax

OUT = 16384
IN = 16384
RANK = 1024
TOKENS = 1024
STEP = 10
N_ROW = 4


def level_of(rng, extent, cuts, smallest, top_value):
    def one(position, parts):
        heights = jax.random.uniform(jax.random.fold_in(jax.random.fold_in(rng, 6), position), (parts,), jnp.float32, smallest / len(cuts), top_value / len(cuts))
        return jnp.repeat(jnp.exp(heights), extent[position] // parts).reshape((-1,) + (1,) * (len(extent) - position - 1))

    level = one(*cuts[0])
    for cut in cuts[1:]:
        level = level * one(*cut)
    return level


def centred(own_key, extent, deviation, bound, cuts=(), kind=jnp.bfloat16):
    drawn = deviation * jax.random.normal(own_key, extent, jnp.float32)
    if cuts:
        drawn = drawn * level_of(own_key, extent, cuts, -0.22, 0.18)
    return jnp.clip(drawn, -bound, bound).astype(kind)


def setup_inputs(seed: int = 0) -> dict:
    keys = jax.random.split(jax.random.key(seed), 7)
    return {
        "grad_out": centred(keys[0], (TOKENS, OUT), (TOKENS ** -0.5), 0.1875, ((0, 8), (1, 4))),
        "activations": centred(keys[1], (TOKENS, IN), 1.0, 6.0, ((0, 4), (1, 8))),
        "projector": centred(keys[2], (OUT, RANK), OUT ** -0.5, 0.046875, ((0, 4),)),
        "weight": centred(keys[3], (OUT, IN), 1.0, 6.0, ((0, 4), (1, 8)), jnp.float32),
        "first_moment": centred(keys[4], (RANK, IN), 0.5, 3.0, ((0, 4), (1, 8)), jnp.float32),
        "second_moment": jnp.clip(jnp.exp(math.log(4.0) - 2.7725887 * jax.random.uniform(keys[5], (RANK, IN), jnp.float32) ** level_of(keys[5], (RANK, IN), ((0, 4), (1, 8)), -0.2, 0.2)), 0.25, 4.0),
    }


first_decay = 0.9
second_decay = 0.99
adam_epsilon = 1e-08
learn_rate = 4.0

def reference(grad_out, activations, projector, weight, first_moment, second_moment):
    block = OUT // N_ROW
    grad_blocks = jnp.transpose(grad_out.reshape(TOKENS, N_ROW, block), (1, 0, 2))
    basis_blocks = projector.reshape(N_ROW, block, RANK)

    def accumulate(carry_sum, pieces):
        grad_block, basis_block = pieces
        tile_grad = lax.dot_general(grad_block, activations, (((0,), (0,)), ((), ())), preferred_element_type=jnp.float32)
        projected = lax.dot_general(basis_block.astype(jnp.float32), tile_grad, (((0,), (0,)), ((), ())), precision=lax.Precision.HIGHEST)
        return (carry_sum + projected, None)
    lowgrad, unused = lax.scan(accumulate, jnp.zeros((RANK, IN), jnp.float32), (grad_blocks, basis_blocks))
    new_first = first_decay * first_moment + (1.0 - first_decay) * lowgrad
    new_second = second_decay * second_moment + (1.0 - second_decay) * lowgrad * lowgrad
    corrected_first = new_first / (1.0 - first_decay ** STEP)
    corrected_second = new_second / (1.0 - second_decay ** STEP)
    direction = corrected_first / (jnp.sqrt(corrected_second) + adam_epsilon)
    update = jnp.dot(projector.astype(jnp.float32), direction, precision=lax.Precision.HIGHEST)
    new_weight = weight - learn_rate * update
    return (new_weight, new_first, new_second)
```

```python
import functools

import jax
import jax.numpy as jnp
from jax import lax
from jax.experimental import pallas as pl
from jax.experimental.pallas import tpu as pltpu
from jax.sharding import PartitionSpec as P

STEP = 10

first_decay = 0.9
second_decay = 0.99
adam_epsilon = 1e-08
learn_rate = 4.0

MIB = 1 << 20
VMEM = pl.BlockSpec(memory_space=pltpu.VMEM)
ANY = pl.BlockSpec(memory_space=pltpu.HBM)
MARK = jax.ShapeDtypeStruct((16, 128), jnp.bfloat16)


def exchange(values, axis, size, mask):
    return lax.ppermute(values, axis, [(i, i ^ mask) for i in range(size)])


def parameters(mib):
    return pltpu.CompilerParams(vmem_limit_bytes=mib * MIB)


def cost(flops, moved):
    return pl.CostEstimate(flops=flops, bytes_accessed=moved, transcendentals=0)


def lowered_kernel(height, cuts, grad_hbm, basis_hbm, input_hbm, *refs):
    n_cuts = len(cuts)
    out_refs, input_refs = refs[: -n_cuts - 4], refs[-n_cuts - 4 : -4]
    grad_ref, basis_ref, total_ref, sems = refs[-4:]
    me = lax.axis_index("row")
    count = basis_ref.shape[0] // height

    def rows(step):
        return slice(step * height, (step + 1) * height)

    copies = [pltpu.make_async_copy(grad_hbm, grad_ref, sems.at[0])]
    for step in range(count):
        copies.append(pltpu.make_async_copy(basis_hbm.at[rows(step)], basis_ref.at[rows(step)], sems.at[1 + step]))
    for index, (at, width) in enumerate(cuts):
        here = slice(at, at + width)
        copies.append(pltpu.make_async_copy(input_hbm.at[:, here], input_refs[index], sems.at[1 + count + index]))
    for copy in copies:
        copy.start()
    copies[0].wait()
    for step in range(count):
        copies[1 + step].wait()
        term = jnp.dot(grad_ref[:, rows(step)], basis_ref[rows(step), :], preferred_element_type=jnp.float32)
        if step == 0:
            total_ref[...] = term
        else:
            total_ref[...] += term
    width = out_refs[0].shape[1]
    for mask, out_ref in enumerate(out_refs):
        columns = pl.ds(pl.multiple_of((me ^ mask) * width, width), width)
        out_ref[...] = total_ref[:, columns].astype(out_ref.dtype)
    for copy in copies[1 + count :]:
        copy.wait()


def lowered_terms(grad_out, projector, activations, cuts, n_row):
    tokens, ranks = grad_out.shape[0], projector.shape[1] // n_row
    height = min(512, projector.shape[0])
    count = projector.shape[0] // height
    kinds = [jnp.float32] + [jnp.bfloat16] * (n_row - 1)
    results = pl.pallas_call(
        functools.partial(lowered_kernel, height, cuts),
        out_shape=[jax.ShapeDtypeStruct((tokens, ranks), kind) for kind in kinds]
        + [pltpu.VMEM((activations.shape[0], width), activations.dtype) for _, width in cuts],
        in_specs=[ANY] * 3,
        out_specs=[VMEM] * (n_row + len(cuts)),
        scratch_shapes=[
            pltpu.VMEM(grad_out.shape, grad_out.dtype),
            pltpu.VMEM(projector.shape, projector.dtype),
            pltpu.VMEM((tokens, projector.shape[1]), jnp.float32),
            pltpu.SemaphoreType.DMA((1 + count + len(cuts),)),
        ],
        compiler_params=parameters(14),
        cost_estimate=cost(1, 1),
        name="lowered_terms",
    )(grad_out, projector, activations)
    return results[:n_row], results[n_row:]


def load_kernel(offset, height, weight_hbm, mark_in, chunk_ref, mark_ref, sems):
    del mark_in
    width = chunk_ref.shape[1]
    copies = []
    for step in range(chunk_ref.shape[0] // height):
        rows = slice(step * height, (step + 1) * height)
        source = weight_hbm.at[rows, offset : offset + width]
        copies.append(pltpu.make_async_copy(source, chunk_ref.at[rows], sems.at[step]))
    for copy in copies:
        copy.start()
    mark_ref[...] = jnp.zeros_like(mark_ref)
    for copy in copies:
        copy.wait()


def load_weight(weight, offset, width, mark):
    rows = weight.shape[0]
    height = min(1024, rows)
    return pl.pallas_call(
        functools.partial(load_kernel, offset, height),
        out_shape=[pltpu.VMEM((rows, width), weight.dtype), MARK],
        in_specs=[ANY, VMEM],
        out_specs=[VMEM, VMEM],
        scratch_shapes=[pltpu.SemaphoreType.DMA((rows // height,))],
        compiler_params=parameters(2),
        cost_estimate=cost(1, 4 * rows * width),
        name="load_weight",
    )(weight, mark)


def share_kernel(n_terms, *refs):
    total = refs[0][...]
    for ref in refs[1:n_terms]:
        total = total + ref[...].astype(jnp.float32)
    refs[-1][...] = total.T.astype(jnp.bfloat16)


def share_sum(terms, marks):
    tokens, ranks = terms[0].shape
    return pl.pallas_call(
        functools.partial(share_kernel, len(terms)),
        out_shape=jax.ShapeDtypeStruct((ranks, tokens), jnp.bfloat16),
        in_specs=[VMEM] * (len(terms) + len(marks)),
        out_specs=VMEM,
        compiler_params=parameters(4),
        cost_estimate=cost(1, 1),
        name="share_sum",
    )(*terms, *marks)


def stack_kernel(n_parts, *refs):
    out_ref, mark_ref = refs[-2:]
    height = refs[0].shape[0]
    for index, part in enumerate(refs[:n_parts]):
        out_ref[index * height : (index + 1) * height] = part[...]
    mark_ref[...] = jnp.zeros_like(mark_ref)


def stack(parts, marks):
    height, width = parts[0].shape
    return pl.pallas_call(
        functools.partial(stack_kernel, len(parts)),
        out_shape=[jax.ShapeDtypeStruct((height * len(parts), width), parts[0].dtype), MARK],
        in_specs=[VMEM] * (len(parts) + len(marks)),
        out_specs=[VMEM, VMEM],
        compiler_params=parameters(4),
        cost_estimate=cost(1, 1),
        name="stack",
    )(*parts, *marks)


def adam_kernel(n_row, n_pieces, n_skip, offset, step, cuts, *refs):
    pieces, refs = refs[:n_pieces], refs[n_pieces:]
    inputs, refs = refs[:n_row], refs[n_row:]
    first_hbm, second_hbm, refs = refs[0], refs[1], refs[2 + n_skip :]
    new_first_ref, new_second_ref, direction_ref, mark_ref = refs[:4]
    part_refs, (lowered_ref, firsts, seconds, sems) = refs[4:-4], refs[-4:]
    mark_ref[...] = jnp.zeros_like(mark_ref)
    depth, width = inputs[0].shape

    def moment_copies(number):
        there = slice(offset + number * step, offset + (number + 1) * step)
        return [
            pltpu.make_async_copy(source.at[:, there], target.at[number], sems.at[number, which])
            for which, (source, target) in enumerate(((first_hbm, firsts), (second_hbm, seconds)))
        ]

    for number in range(width // step):
        for copy in moment_copies(number):
            copy.start()
    row, col = lax.axis_index("row"), lax.axis_index("col")
    ranks, span = lowered_ref.shape[0], pieces[0].shape[1]
    if n_pieces > 1:
        for mask in range(lowered_ref.shape[1] // span):
            columns = pl.ds(pl.multiple_of((col ^ mask) * span, span), span)
            held = pieces[mask % 2]
            lowered_ref[:, columns] = held[mask // 2 * ranks : (mask // 2 + 1) * ranks, :]
    else:
        lowered_ref[...] = pieces[0][...]
    copies = []
    for number, at in enumerate(range(0, width, step)):
        here = slice(at, at + step)
        there = slice(offset + at, offset + at + step)
        lowgrad = None
        for mask, block in enumerate(inputs):
            columns = pl.ds(pl.multiple_of((row ^ mask) * depth, depth), depth)
            term = jnp.dot(lowered_ref[:, columns], block[:, here], preferred_element_type=jnp.float32)
            lowgrad = term if lowgrad is None else lowgrad + term
        for copy in moment_copies(number):
            copy.wait()
        new_first = first_decay * firsts[number] + (1.0 - first_decay) * lowgrad
        new_second = second_decay * seconds[number] + (1.0 - second_decay) * lowgrad * lowgrad
        firsts[number] = new_first
        seconds[number] = new_second
        for which, (source, target) in enumerate(((firsts, new_first_ref), (seconds, new_second_ref))):
            copy = pltpu.make_async_copy(source.at[number], target.at[:, there], sems.at[number, 2 + which])
            copy.start()
            copies.append(copy)
        corrected_first = new_first / (1.0 - first_decay**STEP)
        corrected_second = new_second / (1.0 - second_decay**STEP)
        direction = corrected_first / (jnp.sqrt(corrected_second) + adam_epsilon)
        direction_ref[:, here] = (learn_rate * direction).astype(direction_ref.dtype)
    for (at, width), part_ref in zip(cuts, part_refs):
        part_ref[...] = direction_ref[:, at : at + width]
    for copy in copies:
        copy.wait()


def adam_chunk(pieces, inputs, first, second, marks, carried, offset, cuts, n_row):
    ranks = first.shape[0]
    depth, width = inputs[0].shape
    tokens = depth * n_row
    step = min(256, width)
    count = width // step
    n_plain = len(pieces) + n_row + 2 + len(marks)
    return pl.pallas_call(
        functools.partial(adam_kernel, n_row, len(pieces), len(marks) + len(carried), offset, step, cuts),
        out_shape=[
            jax.ShapeDtypeStruct(first.shape, jnp.float32),
            jax.ShapeDtypeStruct(first.shape, jnp.float32),
            jax.ShapeDtypeStruct((ranks, width), jnp.bfloat16),
            MARK,
            *(jax.ShapeDtypeStruct((ranks, part), jnp.bfloat16) for _, part in cuts),
        ],
        in_specs=[VMEM] * (len(pieces) + n_row) + [ANY] * 2 + [VMEM] * len(marks) + [ANY] * len(carried),
        out_specs=[ANY, ANY, VMEM, VMEM] + [VMEM] * len(cuts),
        scratch_shapes=[
            pltpu.VMEM((ranks, tokens), jnp.bfloat16),
            pltpu.VMEM((count, ranks, step), jnp.float32),
            pltpu.VMEM((count, ranks, step), jnp.float32),
            pltpu.SemaphoreType.DMA((count, 4)),
        ],
        input_output_aliases={n_plain: 0, n_plain + 1: 1} if carried else {},
        compiler_params=parameters(6),
        cost_estimate=cost(1, 1),
        name="adam_chunk",
    )(*pieces, *inputs, first, second, *marks, *carried)


def update_kernel(offset, start, height, slots, n_parts, basis_ref, *refs):
    parts, weight_ref = refs[:n_parts], refs[n_parts]
    out_ref, mark_ref, scaled, held, sems = refs[-5:]
    row = lax.axis_index("row")
    ranks, width = parts[0].shape
    there = slice(offset, offset + width)
    count = weight_ref.shape[0] // height
    for mask, part in enumerate(parts):
        here = slice(start, start + width) if mask == 1 else slice(0, width)
        scaled[pl.ds(pl.multiple_of((row ^ mask) * ranks, ranks), ranks), :] = part[:, here]

    def copy(step):
        slot = step % slots
        rows = slice(step * height, (step + 1) * height)
        return pltpu.make_async_copy(held.at[slot], out_ref.at[rows, there], sems.at[slot])

    for step in range(count):
        if step >= slots:
            copy(step - slots).wait()
        rows = slice(step * height, (step + 1) * height)
        update = jnp.dot(basis_ref[rows, :], scaled[...], preferred_element_type=jnp.float32)
        held[step % slots] = weight_ref[rows, :] - update
        copy(step).start()
    mark_ref[...] = jnp.zeros_like(mark_ref)
    for step in range(max(0, count - slots), count):
        copy(step).wait()


def weight_update(projector, parts, weight, shape, carried, offset, start):
    rows = weight.shape[0]
    ranks, width = parts[0].shape
    height = min(512, rows)
    slots = min(3, rows // height)
    n_parts = len(parts)
    return pl.pallas_call(
        functools.partial(update_kernel, offset, start, height, slots, n_parts),
        out_shape=[jax.ShapeDtypeStruct(shape, jnp.float32), MARK],
        in_specs=[VMEM] * (n_parts + 2) + [ANY] * len(carried),
        out_specs=[ANY, VMEM],
        scratch_shapes=[
            pltpu.VMEM((n_parts * ranks, width), jnp.bfloat16),
            pltpu.VMEM((slots, height, width), jnp.float32),
            pltpu.SemaphoreType.DMA((slots,)),
        ],
        input_output_aliases={n_parts + 2: 0} if carried else {},
        compiler_params=parameters(8),
        cost_estimate=cost(2 * rows * ranks * n_parts * width, 4 * rows * width),
        name="weight_update",
    )(projector, *parts, weight, *carried)


def after_kernel(*refs):
    del refs


def after(parts, *marks):
    return pl.pallas_call(
        after_kernel,
        out_shape=[jax.ShapeDtypeStruct(part.shape, part.dtype) for part in parts],
        in_specs=[VMEM] * (len(parts) + len(marks)),
        out_specs=[VMEM] * len(parts),
        input_output_aliases={i: i for i in range(len(parts))},
        compiler_params=parameters(2),
        cost_estimate=cost(1, 1),
        name="after",
    )(*parts, *marks)


def over_y(values, n_row):
    return [exchange(values, "row", n_row, mask) for mask in range(2, n_row, 2)]


def with_core(far, n_row):
    pieces = []
    for piece in far:
        pieces += [piece, exchange(piece, "row", n_row, 1)]
    return pieces


def cut(total, parts):
    chunks, at = [], 0
    for part in parts:
        width = total * part // 16
        if width % 128:
            return [(0, total)]
        chunks.append((at, width))
        at += width
    return chunks


def body(n_row, n_col, grad_out, activations, projector, weight, first_moment, second_moment):
    grad_out, activations, weight, first_moment, second_moment = [
        pltpu.with_memory_space_constraint(values, pltpu.HBM)
        for values in (grad_out, activations, weight, first_moment, second_moment)
    ]
    halves = cut(activations.shape[1], (8, 8))
    parts_of = [cut(width, (8, 8)) for _, width in halves]
    chunks = [(at + start, width) for (at, _), cuts in zip(halves, parts_of) for start, width in cuts]
    loaded = []

    def load(mark):
        if len(loaded) == len(chunks):
            return []
        loaded.append(load_weight(weight, *chunks[len(loaded)], mark))
        return [loaded[-1][1]]

    basis = pltpu.with_memory_space_constraint(projector, pltpu.HBM)
    terms, inputs = lowered_terms(grad_out, basis, activations, halves, n_row)
    marks = load(terms[1])
    received = [exchange(terms[mask], "row", n_row, mask) for mask in range(1, n_row)]
    inputs = after(inputs, *received)
    far_inputs = [over_y(part, n_row) for part in inputs]
    share = share_sum([terms[0]] + received, marks)
    if n_col == 8:
        marks = load(share)
        near = [share] + [exchange(share, "col", n_col, mask) for mask in (2, 4, 6)]
        near, ready = stack(near, marks)
        pieces = [near, exchange(near, "col", n_col, 1)]
    else:
        pieces, ready = [lax.all_gather(share, "col", axis=1, tiled=True)], share
    marks = load(ready)

    moments, directions = [], []
    for (at, _), cuts, part, far in zip(halves, parts_of, inputs, far_inputs):
        part, *far = after([part, *far], ready)
        gathered = [part, exchange(part, "row", n_row, 1)] + with_core(far, n_row)
        new_first, new_second, direction, ready, *parts = adam_chunk(
            pieces, gathered, first_moment, second_moment, marks, moments, at, cuts, n_row
        )
        moments = [new_first, new_second]
        core = exchange(direction, "row", n_row, 1)
        for (start, _), part in zip(cuts, parts):
            directions.append((start, part, core, over_y(part, n_row)))
        marks = load(ready)

    projector = pltpu.with_memory_space_constraint(projector, pltpu.VMEM)
    new_weight, marks = [], [ready, ready]
    for (at, _), (base, _), (start, part, core, far) in zip(chunks, loaded, directions):
        parts = [part, core] + with_core(after(far, marks[-2]), n_row)
        *new_weight, mark = weight_update(projector, parts, base, weight.shape, new_weight, at, start)
        marks.append(mark)
    return (new_weight[0], *moments)


def solution(mesh):
    n_row, n_col = mesh.shape["row"], mesh.shape["col"]
    in_specs = (
        P("col", "row"),
        P("row", "col"),
        P("row", None),
        P("row", "col"),
        P("row", "col"),
        P("row", "col"),
    )
    out_specs = (P("row", "col"), P("row", "col"), P("row", "col"))
    return jax.shard_map(
        functools.partial(body, n_row, n_col),
        mesh=mesh,
        in_specs=in_specs,
        out_specs=out_specs,
        check_vma=False,
    )
```

```python
import functools

import jax
import jax.numpy as jnp
from jax import lax
from jax.experimental import pallas as pl
from jax.experimental.pallas import tpu as pltpu
from jax.sharding import PartitionSpec as P

STEP = 10

first_decay = 0.9
second_decay = 0.99
adam_epsilon = 1e-08
learn_rate = 4.0

MIB = 1 << 20
VMEM = pl.BlockSpec(memory_space=pltpu.VMEM)
ANY = pl.BlockSpec(memory_space=pltpu.HBM)
MARK = jax.ShapeDtypeStruct((16, 128), jnp.bfloat16)


def exchange(values, axis, size, mask):
    return lax.ppermute(values, axis, [(i, i ^ mask) for i in range(size)])


def parameters(mib):
    return pltpu.CompilerParams(vmem_limit_bytes=mib * MIB)


def cost(flops, moved):
    return pl.CostEstimate(flops=flops, bytes_accessed=moved, transcendentals=0)


def lowered_kernel(height, cuts, grad_hbm, basis_hbm, input_hbm, *refs):
    n_cuts = len(cuts)
    out_refs, whole_ref, input_refs = refs[: -n_cuts - 5], refs[-n_cuts - 5], refs[-n_cuts - 4 : -4]
    grad_ref, basis_ref, total_ref, sems = refs[-4:]
    me = lax.axis_index("row")
    count = basis_ref.shape[0] // height

    def rows(step):
        return slice(step * height, (step + 1) * height)

    copies = [pltpu.make_async_copy(grad_hbm, grad_ref, sems.at[0])]
    for step in range(count):
        copies.append(pltpu.make_async_copy(basis_hbm.at[rows(step)], basis_ref.at[rows(step)], sems.at[1 + step]))
    for index, (at, width) in enumerate(cuts):
        here = slice(at, at + width)
        copies.append(pltpu.make_async_copy(input_hbm.at[:, here], input_refs[index], sems.at[1 + count + index]))
    copies.append(pltpu.make_async_copy(input_hbm, whole_ref, sems.at[1 + count + n_cuts]))
    for copy in copies:
        copy.start()
    copies[0].wait()
    for step in range(count):
        copies[1 + step].wait()
        term = jnp.dot(grad_ref[:, rows(step)], basis_ref[rows(step), :], preferred_element_type=jnp.float32)
        if step == 0:
            total_ref[...] = term
        else:
            total_ref[...] += term
    width = out_refs[0].shape[1]
    for mask, out_ref in enumerate(out_refs):
        columns = pl.ds(pl.multiple_of((me ^ mask) * width, width), width)
        out_ref[...] = total_ref[:, columns].astype(out_ref.dtype)
    for copy in copies[1 + count :]:
        copy.wait()


def lowered_terms(grad_out, projector, activations, cuts, n_row):
    tokens, ranks = grad_out.shape[0], projector.shape[1] // n_row
    height = min(512, projector.shape[0])
    count = projector.shape[0] // height
    kinds = [jnp.float32] + [jnp.bfloat16] * (n_row - 1)
    results = pl.pallas_call(
        functools.partial(lowered_kernel, height, cuts),
        out_shape=[jax.ShapeDtypeStruct((tokens, ranks), kind) for kind in kinds]
        + [pltpu.VMEM((activations.shape[0], width), activations.dtype) for _, width in [(0, activations.shape[1])] + cuts],
        in_specs=[ANY] * 3,
        out_specs=[VMEM] * (n_row + 1 + len(cuts)),
        scratch_shapes=[
            pltpu.VMEM(grad_out.shape, grad_out.dtype),
            pltpu.VMEM(projector.shape, projector.dtype),
            pltpu.VMEM((tokens, projector.shape[1]), jnp.float32),
            pltpu.SemaphoreType.DMA((2 + count + len(cuts),)),
        ],
        compiler_params=parameters(14),
        cost_estimate=cost(1, 1),
        name="lowered_terms",
    )(grad_out, projector, activations)
    return results[:n_row], results[n_row], results[n_row + 1 :]


def load_kernel(cuts, height, weight_hbm, mark_in, *refs):
    del mark_in
    held_refs, mark_ref, sems = refs[:-2], refs[-2], refs[-1]
    copies = []
    for index, (at, width) in enumerate(cuts):
        for step in range(weight_hbm.shape[0] // height):
            rows = slice(step * height, (step + 1) * height)
            source = weight_hbm.at[rows, at : at + width]
            copies.append(pltpu.make_async_copy(source, held_refs[index].at[rows], sems.at[index, step]))
    for copy in copies:
        copy.start()
    mark_ref[...] = jnp.zeros_like(mark_ref)
    for copy in copies:
        copy.wait()


def load_weight(weight, cuts, mark):
    rows = weight.shape[0]
    height = min(1024, rows)
    return pl.pallas_call(
        functools.partial(load_kernel, cuts, height),
        out_shape=[pltpu.VMEM((rows, width), weight.dtype) for _, width in cuts] + [MARK],
        in_specs=[ANY, VMEM],
        out_specs=[VMEM] * (len(cuts) + 1),
        scratch_shapes=[pltpu.SemaphoreType.DMA((len(cuts), rows // height))],
        compiler_params=parameters(2),
        cost_estimate=cost(1, 1),
        name="load_weight",
    )(weight, mark)


def share_kernel(n_terms, *refs):
    total = refs[0][...]
    for ref in refs[1:n_terms]:
        total = total + ref[...].astype(jnp.float32)
    refs[-1][...] = total.T.astype(jnp.bfloat16)


def share_sum(terms, marks):
    tokens, ranks = terms[0].shape
    return pl.pallas_call(
        functools.partial(share_kernel, len(terms)),
        out_shape=jax.ShapeDtypeStruct((ranks, tokens), jnp.bfloat16),
        in_specs=[VMEM] * (len(terms) + len(marks)),
        out_specs=VMEM,
        compiler_params=parameters(4),
        cost_estimate=cost(1, 1),
        name="share_sum",
    )(*terms, *marks)


def stack_kernel(n_parts, *refs):
    out_ref, mark_ref = refs[-2:]
    height = refs[0].shape[0]
    for index, part in enumerate(refs[:n_parts]):
        out_ref[index * height : (index + 1) * height] = part[...]
    mark_ref[...] = jnp.zeros_like(mark_ref)


def stack(parts, marks):
    height, width = parts[0].shape
    return pl.pallas_call(
        functools.partial(stack_kernel, len(parts)),
        out_shape=[jax.ShapeDtypeStruct((height * len(parts), width), parts[0].dtype), MARK],
        in_specs=[VMEM] * (len(parts) + len(marks)),
        out_specs=[VMEM, VMEM],
        compiler_params=parameters(4),
        cost_estimate=cost(1, 1),
        name="stack",
    )(*parts, *marks)


def adam_kernel(counts, n_pieces, n_skip, offset, step, cuts, *refs):
    pieces, refs = refs[:n_pieces], refs[n_pieces:]
    inputs = []
    for count in counts:
        inputs.append(refs[:count])
        refs = refs[count:]
    first_ref, second_ref, refs = refs[0], refs[1], refs[2 + n_skip :]
    new_first_ref, new_second_ref, direction_ref, mark_ref = refs[:4]
    part_refs, (lowered_ref, firsts, seconds, sems) = refs[4:-4], refs[-4:]
    mark_ref[...] = jnp.zeros_like(mark_ref)
    depth, width = inputs[0][0].shape
    row, col = lax.axis_index("row"), lax.axis_index("col")
    ranks, span = lowered_ref.shape[0], pieces[0].shape[1]
    if n_pieces > 1:
        for mask in range(lowered_ref.shape[1] // span):
            columns = pl.ds(pl.multiple_of((col ^ mask) * span, span), span)
            held = pieces[mask % 2]
            lowered_ref[:, columns] = held[mask // 2 * ranks : (mask // 2 + 1) * ranks, :]
    else:
        lowered_ref[...] = pieces[0][...]
    copies = []
    for number, at in enumerate(range(0, width, step)):
        here = slice(at, at + step)
        there = slice(offset + at, offset + at + step)
        lowgrad = None
        for mask, blocks in enumerate(inputs):
            columns = pl.ds(pl.multiple_of((row ^ mask) * depth, depth), depth)
            span = blocks[0].shape[1]
            begin = (offset + at if mask == 1 else at) % span
            block = blocks[0 if mask == 1 else at // span][:, begin : begin + step]
            term = jnp.dot(lowered_ref[:, columns], block, preferred_element_type=jnp.float32)
            lowgrad = term if lowgrad is None else lowgrad + term
        new_first = first_decay * first_ref[:, there] + (1.0 - first_decay) * lowgrad
        new_second = second_decay * second_ref[:, there] + (1.0 - second_decay) * lowgrad * lowgrad
        firsts[number] = new_first
        seconds[number] = new_second
        for which, (source, target) in enumerate(((firsts, new_first_ref), (seconds, new_second_ref))):
            copy = pltpu.make_async_copy(source.at[number], target.at[:, there], sems.at[number, which])
            copy.start()
            copies.append(copy)
        corrected_first = new_first / (1.0 - first_decay**STEP)
        corrected_second = new_second / (1.0 - second_decay**STEP)
        direction = corrected_first / (jnp.sqrt(corrected_second) + adam_epsilon)
        direction_ref[:, here] = (learn_rate * direction).astype(direction_ref.dtype)
    for (at, width), part_ref in zip(cuts, part_refs):
        part_ref[...] = direction_ref[:, at : at + width]
    for copy in copies:
        copy.wait()


def adam_chunk(pieces, inputs, first, second, marks, carried, offset, cuts, n_row):
    ranks = first.shape[0]
    depth, width = inputs[0][0].shape
    tokens = depth * n_row
    counts = [len(blocks) for blocks in inputs]
    step = min(256, width)
    count = width // step
    n_plain = len(pieces) + sum(counts) + 2 + len(marks)
    return pl.pallas_call(
        functools.partial(adam_kernel, counts, len(pieces), len(marks) + len(carried), offset, step, cuts),
        out_shape=[
            jax.ShapeDtypeStruct(first.shape, jnp.float32),
            jax.ShapeDtypeStruct(first.shape, jnp.float32),
            jax.ShapeDtypeStruct((ranks, width), jnp.bfloat16),
            MARK,
            *(jax.ShapeDtypeStruct((ranks, part), jnp.bfloat16) for _, part in cuts),
        ],
        in_specs=[VMEM] * n_plain + [ANY] * len(carried),
        out_specs=[ANY, ANY, VMEM, VMEM] + [VMEM] * len(cuts),
        scratch_shapes=[
            pltpu.VMEM((ranks, tokens), jnp.bfloat16),
            pltpu.VMEM((count, ranks, step), jnp.float32),
            pltpu.VMEM((count, ranks, step), jnp.float32),
            pltpu.SemaphoreType.DMA((count, 2)),
        ],
        input_output_aliases={n_plain: 0, n_plain + 1: 1} if carried else {},
        compiler_params=parameters(6),
        cost_estimate=cost(1, 1),
        name="adam_chunk",
    )(*pieces, *sum(inputs, []), first, second, *marks, *carried)


def gather_pair(pair, parts, start):
    core = lax.rem(lax.axis_index("row"), 2)
    width = pair.shape[1]
    ranks = parts[0][0].shape[0]
    for mask, pieces in enumerate(parts):
        rows = pl.ds(pl.multiple_of((core ^ mask) * ranks, ranks), ranks)
        span = min(width, pieces[0].shape[1])
        for index, piece in enumerate(pieces):
            pair[rows, index * span : (index + 1) * span] = piece[:, start : start + span]


def update_kernel(far_at, start, height, far_counts, n_near, n_far_held, n_near_held, n_skip, basis_ref, *refs):
    far_parts = []
    for count in far_counts:
        far_parts.append(refs[:count])
        refs = refs[count:]
    near_parts = [[part] for part in refs[:n_near]]
    n_held = n_far_held + n_near_held
    refs = refs[n_near + n_held + n_skip :]
    outs, held_refs = refs[: len(refs) - n_held - 3], refs[-n_held - 3 : -3]
    mark_ref, pairs, sems = refs[-3:]
    span = held_refs[0].shape[1]
    count = held_refs[0].shape[0] // height
    ranks = pairs.shape[1] // 2
    chip = lax.axis_index("row") // 2

    def subtract(rows, helds, mask, pair):
        taken = pl.ds(pl.multiple_of((chip ^ mask) * 2 * ranks, 2 * ranks), 2 * ranks)
        update = jnp.dot(basis_ref[rows, taken], pair, preferred_element_type=jnp.float32)
        for index, held in enumerate(helds):
            held[rows, :] = held[rows, :] - update[:, index * span : (index + 1) * span]

    copies = []
    for index in range(0, len(far_parts), 2):
        gather_pair(pairs.at[index // 2 + 1], far_parts[index : index + 2], 0)
    if n_near:
        gather_pair(pairs.at[0], near_parts, start)
    for step in range(count if far_parts else 0):
        rows = slice(step * height, (step + 1) * height)
        for index in range(0, len(far_parts), 2):
            subtract(rows, held_refs[:n_far_held], index // 2 + 1, pairs[index // 2 + 1])
        for index, held in enumerate(held_refs[:n_far_held]):
            target = outs[0].at[rows, far_at + index * span : far_at + (index + 1) * span]
            copies.append(pltpu.make_async_copy(held.at[rows], target, sems.at[step, index]))
            copies[-1].start()
    for step in range(count if n_near else 0):
        rows = slice(step * height, (step + 1) * height)
        subtract(rows, held_refs[n_far_held:], 0, pairs[0])
    mark_ref[...] = jnp.zeros_like(mark_ref)
    for copy in copies:
        copy.wait()


def weight_update(projector, shape, marks, far=(), far_held=(), far_at=0, near=(), near_held=(), start=0, carried=()):
    helds = [*far_held, *near_held]
    counts = [len(pieces) for pieces in far]
    flat = sum(far, []) + list(near)
    rows, span = helds[0].shape
    ranks, width = flat[0].shape[0], span * max(len(far_held), len(near_held))
    height = min(512, rows)
    n_plain = 1 + len(flat)
    out_shape = [jax.ShapeDtypeStruct(shape, jnp.float32)] if far else []
    aliases = {n_plain + index: len(out_shape) + index for index in range(len(helds))}
    if carried:
        aliases[n_plain + len(helds) + len(marks)] = 0
    n_skip = len(marks) + len(carried)
    return pl.pallas_call(
        functools.partial(
            update_kernel, far_at, start, height, counts, len(near), len(far_held), len(near_held), n_skip
        ),
        out_shape=out_shape + [pltpu.VMEM(held.shape, jnp.float32) for held in helds] + [MARK],
        in_specs=[VMEM] * (n_plain + len(helds) + len(marks)) + [ANY] * len(carried),
        out_specs=[ANY] * len(out_shape) + [VMEM] * (len(helds) + 1),
        scratch_shapes=[
            pltpu.VMEM((1 + len(far) // 2, 2 * ranks, width), jnp.bfloat16),
            pltpu.SemaphoreType.DMA((rows // height, max(1, len(far_held)))),
        ],
        input_output_aliases=aliases,
        compiler_params=parameters(6),
        cost_estimate=cost(1, 1),
        name="weight_update",
    )(projector, *flat, *helds, *marks, *carried)


def after_kernel(cuts, n_marks, *refs):
    n_parts = (len(refs) - n_marks) // (2 + len(cuts))
    pieces = refs[2 * n_parts + n_marks :]
    for index in range(n_parts):
        for number, (at, width) in enumerate(cuts):
            pieces[index * len(cuts) + number][...] = refs[index][:, at : at + width]


def after(parts, *marks, cuts=()):
    shapes = [jax.ShapeDtypeStruct(part.shape, part.dtype) for part in parts]
    for part in parts:
        shapes += [jax.ShapeDtypeStruct((part.shape[0], width), part.dtype) for _, width in cuts]
    results = pl.pallas_call(
        functools.partial(after_kernel, cuts, len(marks)),
        out_shape=shapes,
        in_specs=[VMEM] * (len(parts) + len(marks)),
        out_specs=[VMEM] * len(shapes),
        input_output_aliases={i: i for i in range(len(parts))},
        compiler_params=parameters(2),
        cost_estimate=cost(1, 1),
        name="after",
    )(*parts, *marks)
    return results[: len(parts)], results[len(parts) :]


def over_y(values, n_row):
    return [exchange(values, "row", n_row, mask) for mask in range(2, n_row, 2)]


def with_core(far, marks, n_row, pieces):
    cuts = cut(far[0].shape[1], (1,) * pieces)
    far, chunks = after(far, *marks, cuts=cuts)
    parts = []
    for index, part in enumerate(far):
        sent = chunks[index * len(cuts) : (index + 1) * len(cuts)]
        parts += [[part], [exchange(piece, "row", n_row, 1) for piece in sent]]
    return parts


def cut(total, parts):
    unit = total // sum(parts)
    if unit % 128:
        return [(0, total)]
    return [(sum(parts[:index]) * unit, part * unit) for index, part in enumerate(parts)]


def body(n_row, n_col, grad_out, activations, projector, weight, first_moment, second_moment):
    grad_out, activations, weight = [
        pltpu.with_memory_space_constraint(values, pltpu.HBM)
        for values in (grad_out, activations, weight)
    ]
    total = activations.shape[1]
    halves = cut(total, (1, 1))
    parts_of = [cut(width, (1, 1)) for _, width in halves]
    strips = cut(total, (1,) * 8)
    loads = [strips[6:], strips[3:6], strips[:3]]
    held = []

    def load(mark):
        cuts = loads.pop(0)
        if not cuts:
            return []
        *chunks, mark = load_weight(weight, cuts, mark)
        held[:0] = chunks
        return [mark]

    basis = pltpu.with_memory_space_constraint(projector, pltpu.HBM)
    terms, whole, inputs = lowered_terms(grad_out, basis, activations, halves, n_row)
    marks = load(terms[1])
    received = [exchange(terms[mask], "row", n_row, mask) for mask in range(1, n_row)]
    inputs, _ = after(inputs, *received, *marks)
    far_inputs = [over_y(part, n_row) for part in inputs]
    core_input = exchange(whole, "row", n_row, 1)
    share = share_sum([terms[0]] + received, marks)
    if n_col == 8:
        marks = load(share)
        near = [share] + [exchange(share, "col", n_col, mask) for mask in (2, 4, 6)]
        near, ready = stack(near, marks)
        pieces = [near, exchange(near, "col", n_col, 1)]
    else:
        marks = load(share)
        pieces, ready = [lax.all_gather(share, "col", axis=1, tiled=True)], share
    ready = [pieces[-1], *load(ready)]

    moments, chunks = [], []
    for (at, _), cuts, part, far in zip(halves, parts_of, inputs, far_inputs):
        gathered = [[part], [core_input]] + with_core(far, ready, n_row, 2)
        new_first, new_second, direction, mark, *parts = adam_chunk(
            pieces, gathered, first_moment, second_moment, [], moments, at, cuts, n_row
        )
        moments, ready = [new_first, new_second], [mark]
        core = exchange(direction, "row", n_row, 1)
        for (start, width), part in zip(cuts, parts):
            chunks.append((at + start, start, [direction, core], over_y(part, n_row)))

    projector = pltpu.with_memory_space_constraint(projector, pltpu.VMEM)
    each = len(strips) // len(chunks)
    shape = weight.shape
    _, start, near, _ = chunks[0]
    *first_held, mark = weight_update(projector, shape, [], near=near, near_held=held[:each], start=start)
    held[:each] = first_held
    new_weight = []
    for index, (at, _, _, far) in enumerate(chunks):
        far = with_core(far, [mark], n_row, 2)
        here, there = slice(index * each, (index + 1) * each), slice((index + 1) * each, (index + 2) * each)
        _, start, near, _ = chunks[index + 1] if index + 1 < len(chunks) else (0, 0, (), 0)
        new, *moved, mark = weight_update(
            projector, shape, [], far, held[here], at, near, held[there], start, new_weight
        )
        new_weight = [new]
        held[there] = moved[each:]
    return (new_weight[0], *moments)


def solution(mesh):
    n_row, n_col = mesh.shape["row"], mesh.shape["col"]
    in_specs = (
        P("col", "row"),
        P("row", "col"),
        P("row", None),
        P("row", "col"),
        P("row", "col"),
        P("row", "col"),
    )
    out_specs = (P("row", "col"), P("row", "col"), P("row", "col"))
    return jax.shard_map(
        functools.partial(body, n_row, n_col),
        mesh=mesh,
        in_specs=in_specs,
        out_specs=out_specs,
        check_vma=False,
    )
```

```python
import functools

import jax
import jax.numpy as jnp
from jax import lax
from jax.experimental import pallas as pl
from jax.experimental.pallas import tpu as pltpu
from jax.sharding import PartitionSpec as P

STEP = 10

first_decay = 0.9
second_decay = 0.99
adam_epsilon = 1e-08
learn_rate = 4.0

MIB = 1 << 20
VMEM = pl.BlockSpec(memory_space=pltpu.VMEM)
ANY = pl.BlockSpec(memory_space=pltpu.HBM)
MARK = jax.ShapeDtypeStruct((16, 128), jnp.bfloat16)


def exchange(values, axis, size, mask):
    return lax.ppermute(values, axis, [(i, i ^ mask) for i in range(size)])


def parameters(mib):
    return pltpu.CompilerParams(vmem_limit_bytes=mib * MIB)


def cost(flops, moved):
    return pl.CostEstimate(flops=flops, bytes_accessed=moved, transcendentals=0)


def lowered_kernel(height, cuts, grad_hbm, basis_hbm, input_hbm, *refs):
    n_cuts = len(cuts)
    out_refs, whole_ref, input_refs = refs[: -n_cuts - 5], refs[-n_cuts - 5], refs[-n_cuts - 4 : -4]
    grad_ref, basis_ref, total_ref, sems = refs[-4:]
    me = lax.axis_index("row")
    count = basis_ref.shape[0] // height

    def rows(step):
        return slice(step * height, (step + 1) * height)

    copies = [pltpu.make_async_copy(grad_hbm, grad_ref, sems.at[0])]
    for step in range(count):
        copies.append(pltpu.make_async_copy(basis_hbm.at[rows(step)], basis_ref.at[rows(step)], sems.at[1 + step]))
    for index, (at, width) in enumerate(cuts):
        here = slice(at, at + width)
        copies.append(pltpu.make_async_copy(input_hbm.at[:, here], input_refs[index], sems.at[1 + count + index]))
    copies.append(pltpu.make_async_copy(input_hbm, whole_ref, sems.at[1 + count + n_cuts]))
    for copy in copies:
        copy.start()
    copies[0].wait()
    for step in range(count):
        copies[1 + step].wait()
        term = jnp.dot(grad_ref[:, rows(step)], basis_ref[rows(step), :], preferred_element_type=jnp.float32)
        if step == 0:
            total_ref[...] = term
        else:
            total_ref[...] += term
    width = out_refs[0].shape[1]
    for mask, out_ref in enumerate(out_refs):
        columns = pl.ds(pl.multiple_of((me ^ mask) * width, width), width)
        out_ref[...] = total_ref[:, columns].astype(out_ref.dtype)
    for copy in copies[1 + count :]:
        copy.wait()


def lowered_terms(grad_out, projector, activations, cuts, n_row):
    tokens, ranks = grad_out.shape[0], projector.shape[1] // n_row
    height = min(512, projector.shape[0])
    count = projector.shape[0] // height
    kinds = [jnp.float32] + [jnp.bfloat16] * (n_row - 1)
    results = pl.pallas_call(
        functools.partial(lowered_kernel, height, cuts),
        out_shape=[jax.ShapeDtypeStruct((tokens, ranks), kind) for kind in kinds]
        + [pltpu.VMEM((activations.shape[0], width), activations.dtype) for _, width in [(0, activations.shape[1])] + cuts],
        in_specs=[ANY] * 3,
        out_specs=[VMEM] * (n_row + 1 + len(cuts)),
        scratch_shapes=[
            pltpu.VMEM(grad_out.shape, grad_out.dtype),
            pltpu.VMEM(projector.shape, projector.dtype),
            pltpu.VMEM((tokens, projector.shape[1]), jnp.float32),
            pltpu.SemaphoreType.DMA((2 + count + len(cuts),)),
        ],
        compiler_params=parameters(14),
        cost_estimate=cost(1, 1),
        name="lowered_terms",
    )(grad_out, projector, activations)
    return results[:n_row], results[n_row], results[n_row + 1 :]


def load_kernel(cuts, height, weight_hbm, mark_in, *refs):
    del mark_in
    held_refs, mark_ref, sems = refs[:-2], refs[-2], refs[-1]
    copies = []
    for index, (at, width) in enumerate(cuts):
        for step in range(weight_hbm.shape[0] // height):
            rows = slice(step * height, (step + 1) * height)
            source = weight_hbm.at[rows, at : at + width]
            copies.append(pltpu.make_async_copy(source, held_refs[index].at[rows], sems.at[index, step]))
    for copy in copies:
        copy.start()
    mark_ref[...] = jnp.zeros_like(mark_ref)
    for copy in copies:
        copy.wait()


def load_weight(weight, cuts, mark):
    rows = weight.shape[0]
    height = min(1024, rows)
    return pl.pallas_call(
        functools.partial(load_kernel, cuts, height),
        out_shape=[pltpu.VMEM((rows, width), weight.dtype) for _, width in cuts] + [MARK],
        in_specs=[ANY, VMEM],
        out_specs=[VMEM] * (len(cuts) + 1),
        scratch_shapes=[pltpu.SemaphoreType.DMA((len(cuts), rows // height))],
        compiler_params=parameters(2),
        cost_estimate=cost(1, 1),
        name="load_weight",
    )(weight, mark)


def share_kernel(n_terms, *refs):
    total = refs[0][...]
    for ref in refs[1:n_terms]:
        total = total + ref[...].astype(jnp.float32)
    refs[-1][...] = total.T.astype(jnp.bfloat16)


def share_sum(terms, marks):
    tokens, ranks = terms[0].shape
    return pl.pallas_call(
        functools.partial(share_kernel, len(terms)),
        out_shape=jax.ShapeDtypeStruct((ranks, tokens), jnp.bfloat16),
        in_specs=[VMEM] * (len(terms) + len(marks)),
        out_specs=VMEM,
        compiler_params=parameters(4),
        cost_estimate=cost(1, 1),
        name="share_sum",
    )(*terms, *marks)


def stack_kernel(n_parts, *refs):
    out_ref, mark_ref = refs[-2:]
    height = refs[0].shape[0]
    for index, part in enumerate(refs[:n_parts]):
        out_ref[index * height : (index + 1) * height] = part[...]
    mark_ref[...] = jnp.zeros_like(mark_ref)


def stack(parts, marks):
    height, width = parts[0].shape
    return pl.pallas_call(
        functools.partial(stack_kernel, len(parts)),
        out_shape=[jax.ShapeDtypeStruct((height * len(parts), width), parts[0].dtype), MARK],
        in_specs=[VMEM] * (len(parts) + len(marks)),
        out_specs=[VMEM, VMEM],
        compiler_params=parameters(4),
        cost_estimate=cost(1, 1),
        name="stack",
    )(*parts, *marks)


def adam_kernel(counts, n_pieces, n_skip, offset, step, cuts, *refs):
    pieces, refs = refs[:n_pieces], refs[n_pieces:]
    inputs = []
    for count in counts:
        inputs.append(refs[:count])
        refs = refs[count:]
    first_ref, second_ref, refs = refs[0], refs[1], refs[2 + n_skip :]
    new_first_ref, new_second_ref, mark_ref = refs[:3]
    part_refs, (lowered_ref, firsts, seconds, sems) = refs[3:-4], refs[-4:]
    mark_ref[...] = jnp.zeros_like(mark_ref)
    depth, width = inputs[0][0].shape
    row, col = lax.axis_index("row"), lax.axis_index("col")
    ranks, span = lowered_ref.shape[0], pieces[0].shape[1]
    if n_pieces > 1:
        for mask in range(lowered_ref.shape[1] // span):
            columns = pl.ds(pl.multiple_of((col ^ mask) * span, span), span)
            held = pieces[mask % 2]
            lowered_ref[:, columns] = held[mask // 2 * ranks : (mask // 2 + 1) * ranks, :]
    else:
        lowered_ref[...] = pieces[0][...]
    copies = []
    for number, at in enumerate(range(0, width, step)):
        there = slice(offset + at, offset + at + step)
        lowgrad = None
        for mask, blocks in enumerate(inputs):
            columns = pl.ds(pl.multiple_of((row ^ mask) * depth, depth), depth)
            span = blocks[0].shape[1]
            begin = (offset + at if mask == 1 else at) % span
            block = blocks[0 if mask == 1 else at // span][:, begin : begin + step]
            term = jnp.dot(lowered_ref[:, columns], block, preferred_element_type=jnp.float32)
            lowgrad = term if lowgrad is None else lowgrad + term
        new_first = first_decay * first_ref[:, there] + (1.0 - first_decay) * lowgrad
        new_second = second_decay * second_ref[:, there] + (1.0 - second_decay) * lowgrad * lowgrad
        firsts[number] = new_first
        seconds[number] = new_second
        for which, (source, target) in enumerate(((firsts, new_first_ref), (seconds, new_second_ref))):
            copy = pltpu.make_async_copy(source.at[number], target.at[:, there], sems.at[number, which])
            copy.start()
            copies.append(copy)
        corrected_first = new_first / (1.0 - first_decay**STEP)
        corrected_second = new_second / (1.0 - second_decay**STEP)
        direction = corrected_first / (jnp.sqrt(corrected_second) + adam_epsilon)
        for (begin, part_width), part_ref in zip(cuts, part_refs):
            if begin <= at < begin + part_width:
                here = slice(at - begin, at - begin + step)
                part_ref[:, here] = (learn_rate * direction).astype(part_ref.dtype)
    for copy in copies:
        copy.wait()


def adam_chunk(pieces, inputs, first, second, marks, carried, offset, cuts, n_row):
    ranks = first.shape[0]
    depth, width = inputs[0][0].shape
    tokens = depth * n_row
    counts = [len(blocks) for blocks in inputs]
    step = min(256, width)
    count = width // step
    n_plain = len(pieces) + sum(counts) + 2 + len(marks)
    return pl.pallas_call(
        functools.partial(adam_kernel, counts, len(pieces), len(marks) + len(carried), offset, step, cuts),
        out_shape=[
            jax.ShapeDtypeStruct(first.shape, jnp.float32),
            jax.ShapeDtypeStruct(first.shape, jnp.float32),
            MARK,
            *(jax.ShapeDtypeStruct((ranks, part), jnp.bfloat16) for _, part in cuts),
        ],
        in_specs=[VMEM] * n_plain + [ANY] * len(carried),
        out_specs=[ANY, ANY] + [VMEM] * (1 + len(cuts)),
        scratch_shapes=[
            pltpu.VMEM((ranks, tokens), jnp.bfloat16),
            pltpu.VMEM((count, ranks, step), jnp.float32),
            pltpu.VMEM((count, ranks, step), jnp.float32),
            pltpu.SemaphoreType.DMA((count, 2)),
        ],
        input_output_aliases={n_plain: 0, n_plain + 1: 1} if carried else {},
        compiler_params=parameters(6),
        cost_estimate=cost(1, 1),
        name="adam_chunk",
    )(*pieces, *sum(inputs, []), first, second, *marks, *carried)


def gather_pair(pair, parts):
    core = lax.rem(lax.axis_index("row"), 2)
    ranks = parts[0][0].shape[0]
    for mask, pieces in enumerate(parts):
        rows = pl.ds(pl.multiple_of((core ^ mask) * ranks, ranks), ranks)
        span = pieces[0].shape[1]
        for index, piece in enumerate(pieces):
            pair[rows, index * span : (index + 1) * span] = piece[...]


def update_kernel(far_at, height, near_steps, masks, final, counts, n_near, n_far_held, n_near_held, n_skip, basis_ref, *refs):
    far_parts = []
    for count in counts:
        far_parts.append(refs[:count])
        refs = refs[count:]
    near_parts, far_parts = far_parts[:n_near], far_parts[n_near:]
    n_held = n_far_held + n_near_held
    refs = refs[n_held + n_skip :]
    outs, held_refs = refs[: len(refs) - n_held - 3], refs[-n_held - 3 : -3]
    mark_ref, pairs, sems = refs[-3:]
    span = held_refs[0].shape[1]
    count = held_refs[0].shape[0] // height
    ranks = pairs.shape[1] // 2
    chip = lax.axis_index("row") // 2

    def subtract(rows, helds, first, depth, pair):
        taken = pl.ds(pl.multiple_of(first * depth, depth), depth)
        update = jnp.dot(basis_ref[rows, taken], pair, preferred_element_type=jnp.float32)
        for index, held in enumerate(helds):
            held[rows, :] = held[rows, :] - update[:, index * span : (index + 1) * span]

    copies = []
    row = lax.axis_index("row")
    terms = []
    for index in range(0, len(far_parts), 1 if masks else 2):
        if masks:
            span_in = far_parts[index][0].shape[1]
            for number, piece in enumerate(far_parts[index]):
                pairs[index + 1, :ranks, number * span_in : (number + 1) * span_in] = piece[...]
            terms.append((row ^ masks[index], ranks, pairs.at[index + 1, :ranks]))
        else:
            gather_pair(pairs.at[index // 2 + 1], far_parts[index : index + 2])
            terms.append((chip ^ (index // 2 + 1), 2 * ranks, pairs.at[index // 2 + 1]))
    if n_near:
        gather_pair(pairs.at[0], near_parts)
    for step in range(count if far_parts else 0):
        rows = slice(step * height, (step + 1) * height)
        for first, depth, pair in terms:
            subtract(rows, held_refs[:n_far_held], first, depth, pair[...])
        for index, held in enumerate(held_refs[:n_far_held] if final else ()):
            target = outs[0].at[rows, far_at + index * span : far_at + (index + 1) * span]
            copies.append(pltpu.make_async_copy(held.at[rows], target, sems.at[step, index]))
            copies[-1].start()
    for step in near_steps:
        rows = slice(step * height, (step + 1) * height)
        subtract(rows, held_refs[n_far_held:], chip, 2 * ranks, pairs[0])
    mark_ref[...] = jnp.zeros_like(mark_ref)
    for copy in copies:
        copy.wait()


def weight_update(projector, shape, marks, far=(), far_held=(), far_at=0, near=(), near_held=(), part=(0, 1), masks=(), final=True, carried=()):
    helds = [*far_held, *near_held]
    counts = [len(pieces) for pieces in [*near, *far]]
    flat = sum([*near, *far], [])
    rows, span = helds[0].shape
    ranks, width = flat[0].shape[0], span * max(len(far_held), len(near_held))
    height = min(512, rows)
    begin, end = (int(edge * (rows // height)) for edge in part)
    near_steps = range(begin, end) if near else ()
    n_plain = 1 + len(flat)
    final = final and bool(far)
    out_shape = [jax.ShapeDtypeStruct(shape, jnp.float32)] if final else []
    aliases = {n_plain + index: len(out_shape) + index for index in range(len(helds))}
    if carried:
        aliases[n_plain + len(helds) + len(marks)] = 0
    n_skip = len(marks) + len(carried)
    return pl.pallas_call(
        functools.partial(
            update_kernel, far_at, height, near_steps, masks, final, counts, len(near), len(far_held), len(near_held), n_skip
        ),
        out_shape=out_shape + [pltpu.VMEM(held.shape, jnp.float32) for held in helds] + [MARK],
        in_specs=[VMEM] * (n_plain + len(helds) + len(marks)) + [ANY] * len(carried),
        out_specs=[ANY] * len(out_shape) + [VMEM] * (len(helds) + 1),
        scratch_shapes=[
            pltpu.VMEM((1 + (len(far) if masks else len(far) // 2), 2 * ranks, width), jnp.bfloat16),
            pltpu.SemaphoreType.DMA((rows // height, max(1, len(far_held)))),
        ],
        input_output_aliases=aliases,
        compiler_params=parameters(6),
        cost_estimate=cost(1, 1),
        name="weight_update",
    )(projector, *flat, *helds, *marks, *carried)


def after_kernel(cuts, n_marks, *refs):
    n_parts = (len(refs) - n_marks) // (2 + len(cuts))
    pieces = refs[2 * n_parts + n_marks :]
    for index in range(n_parts):
        for number, (at, width) in enumerate(cuts):
            pieces[index * len(cuts) + number][...] = refs[index][:, at : at + width]


def after(parts, *marks, cuts=()):
    shapes = [jax.ShapeDtypeStruct(part.shape, part.dtype) for part in parts]
    for part in parts:
        shapes += [jax.ShapeDtypeStruct((part.shape[0], width), part.dtype) for _, width in cuts]
    results = pl.pallas_call(
        functools.partial(after_kernel, cuts, len(marks)),
        out_shape=shapes,
        in_specs=[VMEM] * (len(parts) + len(marks)),
        out_specs=[VMEM] * len(shapes),
        input_output_aliases={i: i for i in range(len(parts))},
        compiler_params=parameters(2),
        cost_estimate=cost(1, 1),
        name="after",
    )(*parts, *marks)
    return results[: len(parts)], results[len(parts) :]


def over_y(values, n_row):
    return [exchange(values, "row", n_row, mask) for mask in range(2, n_row, 2)]


def with_core(far, marks, n_row, pieces):
    cuts = cut(far[0].shape[1], (1,) * pieces)
    far, chunks = after(far, *marks, cuts=cuts)
    parts = []
    for index, part in enumerate(far):
        sent = chunks[index * len(cuts) : (index + 1) * len(cuts)]
        parts += [[part], [exchange(piece, "row", n_row, 1) for piece in sent]]
    return parts


def cut(total, parts):
    unit = total // sum(parts)
    if unit % 128:
        return [(0, total)]
    return [(sum(parts[:index]) * unit, part * unit) for index, part in enumerate(parts)]


def body(n_row, n_col, grad_out, activations, projector, weight, first_moment, second_moment):
    grad_out, activations, weight = [
        pltpu.with_memory_space_constraint(values, pltpu.HBM)
        for values in (grad_out, activations, weight)
    ]
    total = activations.shape[1]
    halves = cut(total, (1, 1))
    parts_of = [[(0, halves[0][1])] + cut(halves[0][1], (1,) * pieces) for pieces in (2, 4)]
    strips = cut(total, (1,) * 8)
    loads = [strips[6:], strips[3:6], strips[:3]]
    held = []

    def load(mark):
        cuts = loads.pop(0)
        if not cuts:
            return []
        *chunks, mark = load_weight(weight, cuts, mark)
        held[:0] = chunks
        return [mark]

    basis = pltpu.with_memory_space_constraint(projector, pltpu.HBM)
    terms, whole, inputs = lowered_terms(grad_out, basis, activations, halves, n_row)
    marks = load(terms[1])
    received = [exchange(terms[mask], "row", n_row, mask) for mask in range(1, n_row)]
    inputs, _ = after(inputs, *received, *marks)
    far_inputs = [over_y(part, n_row) for part in inputs]
    core_input = exchange(whole, "row", n_row, 1)
    share = share_sum([terms[0]] + received, marks)
    if n_col == 8:
        marks = load(share)
        near = [share] + [exchange(share, "col", n_col, mask) for mask in (2, 4, 6)]
        near, ready = stack(near, marks)
        pieces = [near, exchange(near, "col", n_col, 1)]
    else:
        marks = load(share)
        pieces, ready = [lax.all_gather(share, "col", axis=1, tiled=True)], share
    ready = [pieces[-1], *load(ready)]

    projector = pltpu.with_memory_space_constraint(projector, pltpu.VMEM)
    each, shape = len(strips) // len(halves), weight.shape
    moments, chunks, marks = [], [], []
    for (at, _), cuts, part, far in zip(halves, parts_of, inputs, far_inputs):
        gathered = [[part], [core_input]] + with_core(far, ready, n_row, 4 if moments else 2)
        new_first, new_second, mark, direction, *parts = adam_chunk(
            pieces, gathered, first_moment, second_moment, marks, moments, at, cuts, n_row
        )
        moments, ready = [new_first, new_second], [mark]
        here = slice(len(chunks) * each, (len(chunks) + 1) * each)
        near = [[direction], [exchange(part, "row", n_row, 1) for part in parts]]
        chunks.append((at, here, near, over_y(direction, n_row)))
        if len(chunks) > 1:
            before, part = chunks[-2][1], (0.5, 1)
            *held[before], mark = weight_update(
                projector, shape, ready, near=chunks[-2][2], near_held=held[before], part=part
            )
            ready = [mark]
        *held[here], mark = weight_update(
            projector, shape, ready, near=near, near_held=held[here], part=(0, 0.5)
        )
        marks = [mark]

    new_weight = []
    for index, (at, here, near, far) in enumerate(chunks):
        far = with_core(far, marks, n_row, 2)
        if not index:
            last = chunks[-1][1]
            *held[last], mark = weight_update(
                projector, shape, marks, near=chunks[-1][2], near_held=held[last], part=(0.5, 1)
            )
            marks = [mark]
        masks = ()
        if index and index == len(chunks) - 1:
            *held[here], mark = weight_update(
                projector, shape, marks, far[0::2], held[here], masks=range(2, n_row, 2), final=False
            )
            marks, far, masks = [mark], far[1::2], range(3, n_row, 2)
        new, *_, mark = weight_update(
            projector, shape, marks, far, held[here], at, masks=masks, carried=new_weight
        )
        new_weight, marks = [new], [mark]
    return (new_weight[0], *moments)


def solution(mesh):
    n_row, n_col = mesh.shape["row"], mesh.shape["col"]
    in_specs = (
        P("col", "row"),
        P("row", "col"),
        P("row", None),
        P("row", "col"),
        P("row", "col"),
        P("row", "col"),
    )
    out_specs = (P("row", "col"), P("row", "col"), P("row", "col"))
    return jax.shard_map(
        functools.partial(body, n_row, n_col),
        mesh=mesh,
        in_specs=in_specs,
        out_specs=out_specs,
        check_vma=False,
    )
```

```python
import functools

import jax
import jax.numpy as jnp
from jax import lax
from jax.experimental import pallas as pl
from jax.experimental.pallas import tpu as pltpu
from jax.sharding import PartitionSpec as P

STEP = 10

first_decay = 0.9
second_decay = 0.99
adam_epsilon = 1e-08
learn_rate = 4.0

MIB = 1 << 20
VMEM = pl.BlockSpec(memory_space=pltpu.VMEM)
ANY = pl.BlockSpec(memory_space=pltpu.HBM)
MARK = jax.ShapeDtypeStruct((16, 128), jnp.bfloat16)


def exchange(values, axis, size, mask):
    return lax.ppermute(values, axis, [(i, i ^ mask) for i in range(size)])


def parameters(mib):
    return pltpu.CompilerParams(vmem_limit_bytes=mib * MIB)


def cost(flops, moved):
    return pl.CostEstimate(flops=flops, bytes_accessed=moved, transcendentals=0)


def lowered_kernel(height, cuts, grad_hbm, basis_hbm, input_hbm, *refs):
    n_cuts = len(cuts)
    out_refs, whole_ref, input_refs = refs[: -n_cuts - 5], refs[-n_cuts - 5], refs[-n_cuts - 4 : -4]
    grad_ref, basis_ref, total_ref, sems = refs[-4:]
    me = lax.axis_index("row")
    count = basis_ref.shape[0] // height

    def rows(step):
        return slice(step * height, (step + 1) * height)

    copies = [pltpu.make_async_copy(grad_hbm, grad_ref, sems.at[0])]
    for step in range(count):
        copies.append(pltpu.make_async_copy(basis_hbm.at[rows(step)], basis_ref.at[rows(step)], sems.at[1 + step]))
    for index, (at, width) in enumerate(cuts):
        here = slice(at, at + width)
        copies.append(pltpu.make_async_copy(input_hbm.at[:, here], input_refs[index], sems.at[1 + count + index]))
    copies.append(pltpu.make_async_copy(input_hbm, whole_ref, sems.at[1 + count + n_cuts]))
    for copy in copies:
        copy.start()
    copies[0].wait()
    for step in range(count):
        copies[1 + step].wait()
        term = jnp.dot(grad_ref[:, rows(step)], basis_ref[rows(step), :], preferred_element_type=jnp.float32)
        if step == 0:
            total_ref[...] = term
        else:
            total_ref[...] += term
    width = out_refs[0].shape[1]
    for mask, out_ref in enumerate(out_refs):
        columns = pl.ds(pl.multiple_of((me ^ mask) * width, width), width)
        out_ref[...] = total_ref[:, columns].astype(out_ref.dtype)
    for copy in copies[1 + count :]:
        copy.wait()


def lowered_terms(grad_out, projector, activations, cuts, n_row):
    tokens, ranks = grad_out.shape[0], projector.shape[1] // n_row
    height = min(512, projector.shape[0])
    count = projector.shape[0] // height
    kinds = [jnp.float32] + [jnp.bfloat16] * (n_row - 1)
    results = pl.pallas_call(
        functools.partial(lowered_kernel, height, cuts),
        out_shape=[jax.ShapeDtypeStruct((tokens, ranks), kind) for kind in kinds]
        + [pltpu.VMEM((activations.shape[0], width), activations.dtype) for _, width in [(0, activations.shape[1])] + cuts],
        in_specs=[ANY] * 3,
        out_specs=[VMEM] * (n_row + 1 + len(cuts)),
        scratch_shapes=[
            pltpu.VMEM(grad_out.shape, grad_out.dtype),
            pltpu.VMEM(projector.shape, projector.dtype),
            pltpu.VMEM((tokens, projector.shape[1]), jnp.float32),
            pltpu.SemaphoreType.DMA((2 + count + len(cuts),)),
        ],
        compiler_params=parameters(14),
        cost_estimate=cost(1, 1),
        name="lowered_terms",
    )(grad_out, projector, activations)
    return results[:n_row], results[n_row], results[n_row + 1 :]


def load_kernel(cuts, height, weight_hbm, mark_in, *refs):
    del mark_in
    held_refs, mark_ref, sems = refs[:-2], refs[-2], refs[-1]
    copies = []
    for index, (at, width) in enumerate(cuts):
        for step in range(weight_hbm.shape[0] // height):
            rows = slice(step * height, (step + 1) * height)
            source = weight_hbm.at[rows, at : at + width]
            copies.append(pltpu.make_async_copy(source, held_refs[index].at[rows], sems.at[index, step]))
    for copy in copies:
        copy.start()
    mark_ref[...] = jnp.zeros_like(mark_ref)
    for copy in copies:
        copy.wait()


def load_weight(weight, cuts, mark):
    rows = weight.shape[0]
    height = min(1024, rows)
    return pl.pallas_call(
        functools.partial(load_kernel, cuts, height),
        out_shape=[pltpu.VMEM((rows, width), weight.dtype) for _, width in cuts] + [MARK],
        in_specs=[ANY, VMEM],
        out_specs=[VMEM] * (len(cuts) + 1),
        scratch_shapes=[pltpu.SemaphoreType.DMA((len(cuts), rows // height))],
        compiler_params=parameters(2),
        cost_estimate=cost(1, 1),
        name="load_weight",
    )(weight, mark)


def share_kernel(n_terms, *refs):
    total = refs[0][...]
    for ref in refs[1:n_terms]:
        total = total + ref[...].astype(jnp.float32)
    refs[-1][...] = total.T.astype(jnp.bfloat16)


def share_sum(terms, marks):
    tokens, ranks = terms[0].shape
    return pl.pallas_call(
        functools.partial(share_kernel, len(terms)),
        out_shape=jax.ShapeDtypeStruct((ranks, tokens), jnp.bfloat16),
        in_specs=[VMEM] * (len(terms) + len(marks)),
        out_specs=VMEM,
        compiler_params=parameters(4),
        cost_estimate=cost(1, 1),
        name="share_sum",
    )(*terms, *marks)


def stack_kernel(n_parts, *refs):
    out_ref, mark_ref = refs[-2:]
    height = refs[0].shape[0]
    for index, part in enumerate(refs[:n_parts]):
        out_ref[index * height : (index + 1) * height] = part[...]
    mark_ref[...] = jnp.zeros_like(mark_ref)


def stack(parts, marks):
    height, width = parts[0].shape
    return pl.pallas_call(
        functools.partial(stack_kernel, len(parts)),
        out_shape=[jax.ShapeDtypeStruct((height * len(parts), width), parts[0].dtype), MARK],
        in_specs=[VMEM] * (len(parts) + len(marks)),
        out_specs=[VMEM, VMEM],
        compiler_params=parameters(4),
        cost_estimate=cost(1, 1),
        name="stack",
    )(*parts, *marks)


def adam_kernel(counts, n_pieces, n_skip, offset, step, cuts, *refs):
    pieces, refs = refs[:n_pieces], refs[n_pieces:]
    inputs = []
    for count in counts:
        inputs.append(refs[:count])
        refs = refs[count:]
    first_ref, second_ref, refs = refs[0], refs[1], refs[2 + n_skip :]
    new_first_ref, new_second_ref, mark_ref = refs[:3]
    part_refs, (lowered_ref, firsts, seconds, sems) = refs[3:-4], refs[-4:]
    mark_ref[...] = jnp.zeros_like(mark_ref)
    depth, width = inputs[0][0].shape
    row, col = lax.axis_index("row"), lax.axis_index("col")
    ranks, span = lowered_ref.shape[0], pieces[0].shape[1]
    if n_pieces > 1:
        for mask in range(lowered_ref.shape[1] // span):
            columns = pl.ds(pl.multiple_of((col ^ mask) * span, span), span)
            held = pieces[mask % 2]
            lowered_ref[:, columns] = held[mask // 2 * ranks : (mask // 2 + 1) * ranks, :]
    else:
        lowered_ref[...] = pieces[0][...]
    copies = []
    for number, at in enumerate(range(0, width, step)):
        there = slice(offset + at, offset + at + step)
        lowgrad = None
        for mask, blocks in enumerate(inputs):
            columns = pl.ds(pl.multiple_of((row ^ mask) * depth, depth), depth)
            span = blocks[0].shape[1]
            begin = (offset + at if mask == 1 else at) % span
            block = blocks[0 if mask == 1 else at // span][:, begin : begin + step]
            term = jnp.dot(lowered_ref[:, columns], block, preferred_element_type=jnp.float32)
            lowgrad = term if lowgrad is None else lowgrad + term
        new_first = first_decay * first_ref[:, there] + (1.0 - first_decay) * lowgrad
        new_second = second_decay * second_ref[:, there] + (1.0 - second_decay) * lowgrad * lowgrad
        firsts[number] = new_first
        seconds[number] = new_second
        for which, (source, target) in enumerate(((firsts, new_first_ref), (seconds, new_second_ref))):
            copy = pltpu.make_async_copy(source.at[number], target.at[:, there], sems.at[number, which])
            copy.start()
            copies.append(copy)
        corrected_first = new_first / (1.0 - first_decay**STEP)
        corrected_second = new_second / (1.0 - second_decay**STEP)
        direction = corrected_first / (jnp.sqrt(corrected_second) + adam_epsilon)
        for (begin, part_width), part_ref in zip(cuts, part_refs):
            if begin <= at < begin + part_width:
                here = slice(at - begin, at - begin + step)
                part_ref[:, here] = (learn_rate * direction).astype(part_ref.dtype)
    for copy in copies:
        copy.wait()


def adam_chunk(pieces, inputs, first, second, marks, carried, offset, cuts, n_row):
    ranks = first.shape[0]
    depth, width = inputs[0][0].shape
    tokens = depth * n_row
    counts = [len(blocks) for blocks in inputs]
    step = min(256, width)
    count = width // step
    n_plain = len(pieces) + sum(counts) + 2 + len(marks)
    return pl.pallas_call(
        functools.partial(adam_kernel, counts, len(pieces), len(marks) + len(carried), offset, step, cuts),
        out_shape=[
            jax.ShapeDtypeStruct(first.shape, jnp.float32),
            jax.ShapeDtypeStruct(first.shape, jnp.float32),
            MARK,
            *(jax.ShapeDtypeStruct((ranks, part), jnp.bfloat16) for _, part in cuts),
        ],
        in_specs=[VMEM] * n_plain + [ANY] * len(carried),
        out_specs=[ANY, ANY] + [VMEM] * (1 + len(cuts)),
        scratch_shapes=[
            pltpu.VMEM((ranks, tokens), jnp.bfloat16),
            pltpu.VMEM((count, ranks, step), jnp.float32),
            pltpu.VMEM((count, ranks, step), jnp.float32),
            pltpu.SemaphoreType.DMA((count, 2)),
        ],
        input_output_aliases={n_plain: 0, n_plain + 1: 1} if carried else {},
        compiler_params=parameters(6),
        cost_estimate=cost(1, 1),
        name="adam_chunk",
    )(*pieces, *sum(inputs, []), first, second, *marks, *carried)


def gather_pair(pair, parts):
    core = lax.rem(lax.axis_index("row"), 2)
    ranks = parts[0][0].shape[0]
    for mask, pieces in enumerate(parts):
        rows = pl.ds(pl.multiple_of((core ^ mask) * ranks, ranks), ranks)
        span = pieces[0].shape[1]
        for index, piece in enumerate(pieces):
            pair[rows, index * span : (index + 1) * span] = piece[...]


def update_kernel(far_at, height, steps, late, masks, final, counts, n_near, n_far_held, n_near_held, n_skip, basis_ref, *refs):
    far_parts = []
    for count in counts:
        far_parts.append(refs[:count])
        refs = refs[count:]
    near_parts, far_parts = far_parts[:n_near], far_parts[n_near:]
    n_held = n_far_held + n_near_held
    refs = refs[n_held + n_skip :]
    outs, held_refs = refs[: len(refs) - n_held - 3], refs[-n_held - 3 : -3]
    mark_ref, pairs, sems = refs[-3:]
    span = held_refs[0].shape[1]
    count = held_refs[0].shape[0] // height
    ranks = pairs.shape[1] // 2
    chip = lax.axis_index("row") // 2

    def subtract(rows, helds, first, depth, pair):
        taken = pl.ds(pl.multiple_of(first * depth, depth), depth)
        update = jnp.dot(basis_ref[rows, taken], pair, preferred_element_type=jnp.float32)
        for index, held in enumerate(helds):
            held[rows, :] = held[rows, :] - update[:, index * span : (index + 1) * span]

    copies = []
    row = lax.axis_index("row")
    terms = []
    for index in range(0, len(far_parts), 1 if masks else 2):
        if masks:
            span_in = far_parts[index][0].shape[1]
            for number, piece in enumerate(far_parts[index]):
                pairs[index + 1, :ranks, number * span_in : (number + 1) * span_in] = piece[...]
            terms.append((row ^ masks[index], ranks, pairs.at[index + 1, :ranks]))
        else:
            gather_pair(pairs.at[index // 2 + 1], far_parts[index : index + 2])
            terms.append((chip ^ (index // 2 + 1), 2 * ranks, pairs.at[index // 2 + 1]))
    if n_near:
        gather_pair(pairs.at[0], near_parts)
    for step in (range(count) if final else steps if far_parts else ()):
        rows = slice(step * height, (step + 1) * height)
        for first, depth, pair in terms[late if step in steps else 0 :]:
            subtract(rows, held_refs[:n_far_held], first, depth, pair[...])
        for index, held in enumerate(held_refs[:n_far_held] if final else ()):
            target = outs[0].at[rows, far_at + index * span : far_at + (index + 1) * span]
            copies.append(pltpu.make_async_copy(held.at[rows], target, sems.at[step, index]))
            copies[-1].start()
    for step in steps if n_near else ():
        rows = slice(step * height, (step + 1) * height)
        subtract(rows, held_refs[n_far_held:], chip, 2 * ranks, pairs[0])
    mark_ref[...] = jnp.zeros_like(mark_ref)
    for copy in copies:
        copy.wait()


def weight_update(projector, shape, marks, far=(), far_held=(), far_at=0, near=(), near_held=(), part=(0, 1), masks=(), late=0, final=True, carried=()):
    helds = [*far_held, *near_held]
    counts = [len(pieces) for pieces in [*near, *far]]
    flat = sum([*near, *far], [])
    rows, span = helds[0].shape
    ranks, width = flat[0].shape[0], span * max(len(far_held), len(near_held))
    height = min(512, rows)
    begin, end = (int(edge * (rows // height)) for edge in part)
    steps = range(begin, end)
    n_plain = 1 + len(flat)
    final = final and bool(far)
    out_shape = [jax.ShapeDtypeStruct(shape, jnp.float32)] if final else []
    aliases = {n_plain + index: len(out_shape) + index for index in range(len(helds))}
    if carried:
        aliases[n_plain + len(helds) + len(marks)] = 0
    n_skip = len(marks) + len(carried)
    return pl.pallas_call(
        functools.partial(
            update_kernel, far_at, height, steps, late, masks, final, counts, len(near), len(far_held), len(near_held), n_skip
        ),
        out_shape=out_shape + [pltpu.VMEM(held.shape, jnp.float32) for held in helds] + [MARK],
        in_specs=[VMEM] * (n_plain + len(helds) + len(marks)) + [ANY] * len(carried),
        out_specs=[ANY] * len(out_shape) + [VMEM] * (len(helds) + 1),
        scratch_shapes=[
            pltpu.VMEM((1 + (len(far) if masks else len(far) // 2), 2 * ranks, width), jnp.bfloat16),
            pltpu.SemaphoreType.DMA((rows // height, max(1, len(far_held)))),
        ],
        input_output_aliases=aliases,
        compiler_params=parameters(6),
        cost_estimate=cost(1, 1),
        name="weight_update",
    )(projector, *flat, *helds, *marks, *carried)


def after_kernel(cuts, n_marks, *refs):
    n_parts = (len(refs) - n_marks) // (2 + len(cuts))
    pieces = refs[2 * n_parts + n_marks :]
    for index in range(n_parts):
        for number, (at, width) in enumerate(cuts):
            pieces[index * len(cuts) + number][...] = refs[index][:, at : at + width]


def after(parts, *marks, cuts=()):
    shapes = [jax.ShapeDtypeStruct(part.shape, part.dtype) for part in parts]
    for part in parts:
        shapes += [jax.ShapeDtypeStruct((part.shape[0], width), part.dtype) for _, width in cuts]
    results = pl.pallas_call(
        functools.partial(after_kernel, cuts, len(marks)),
        out_shape=shapes,
        in_specs=[VMEM] * (len(parts) + len(marks)),
        out_specs=[VMEM] * len(shapes),
        input_output_aliases={i: i for i in range(len(parts))},
        compiler_params=parameters(2),
        cost_estimate=cost(1, 1),
        name="after",
    )(*parts, *marks)
    return results[: len(parts)], results[len(parts) :]


def over_y(values, n_row):
    return [exchange(values, "row", n_row, mask) for mask in range(2, n_row, 2)]


def with_core(far, marks, n_row, pieces):
    cuts = cut(far[0].shape[1], (1,) * pieces)
    far, chunks = after(far, *marks, cuts=cuts)
    parts = []
    for index, part in enumerate(far):
        sent = chunks[index * len(cuts) : (index + 1) * len(cuts)]
        parts += [[part], [exchange(piece, "row", n_row, 1) for piece in sent]]
    return parts


def cut(total, parts):
    unit = total // sum(parts)
    if unit % 128:
        return [(0, total)]
    return [(sum(parts[:index]) * unit, part * unit) for index, part in enumerate(parts)]


def body(n_row, n_col, grad_out, activations, projector, weight, first_moment, second_moment):
    grad_out, activations, weight = [
        pltpu.with_memory_space_constraint(values, pltpu.HBM)
        for values in (grad_out, activations, weight)
    ]
    total = activations.shape[1]
    halves = cut(total, (1, 1))
    parts_of = [[(0, halves[0][1])] + cut(halves[0][1], (1,) * pieces) for pieces in (2, 4)]
    strips = cut(total, (1,) * 8)
    loads = [strips[6:], strips[3:6], strips[:3]]
    held = []

    def load(mark):
        cuts = loads.pop(0)
        if not cuts:
            return []
        *chunks, mark = load_weight(weight, cuts, mark)
        held[:0] = chunks
        return [mark]

    basis = pltpu.with_memory_space_constraint(projector, pltpu.HBM)
    terms, whole, inputs = lowered_terms(grad_out, basis, activations, halves, n_row)
    marks = load(terms[1])
    received = [exchange(terms[mask], "row", n_row, mask) for mask in range(1, n_row)]
    inputs, _ = after(inputs, *received, *marks)
    far_inputs = [over_y(part, n_row) for part in inputs]
    core_input = exchange(whole, "row", n_row, 1)
    share = share_sum([terms[0]] + received, marks)
    if n_col == 8:
        marks = load(share)
        near = [share] + [exchange(share, "col", n_col, mask) for mask in (2, 4, 6)]
        near, ready = stack(near, marks)
        pieces = [near, exchange(near, "col", n_col, 1)]
    else:
        marks = load(share)
        pieces, ready = [lax.all_gather(share, "col", axis=1, tiled=True)], share
    ready = [pieces[-1], *load(ready)]

    projector = pltpu.with_memory_space_constraint(projector, pltpu.VMEM)
    each, shape = len(strips) // len(halves), weight.shape
    moments, chunks, marks = [], [], []
    for (at, _), cuts, part, far in zip(halves, parts_of, inputs, far_inputs):
        gathered = [[part], [core_input]] + with_core(far, ready, n_row, 4 if moments else 2)
        new_first, new_second, mark, direction, *parts = adam_chunk(
            pieces, gathered, first_moment, second_moment, marks, moments, at, cuts, n_row
        )
        moments, ready = [new_first, new_second], [mark]
        here = slice(len(chunks) * each, (len(chunks) + 1) * each)
        near = [[direction], [exchange(part, "row", n_row, 1) for part in parts]]
        chunks.append((at, here, near, over_y(direction, n_row)))
        if len(chunks) > 1:
            before, part = chunks[-2][1], (0.5, 1)
            *held[before], mark = weight_update(
                projector, shape, ready, near=chunks[-2][2], near_held=held[before], part=part
            )
            ready = [mark]
        *held[here], mark = weight_update(
            projector, shape, ready, near=near, near_held=held[here], part=(0, 0.5)
        )
        marks = [mark]

    new_weight = []
    for index, (at, here, near, far) in enumerate(chunks):
        far = with_core(far, marks, n_row, 2)
        if not index:
            last = chunks[-1][1]
            *held[last], mark = weight_update(
                projector, shape, marks, near=chunks[-1][2], near_held=held[last], part=(0.5, 1)
            )
            marks = [mark]
        masks, late = (), 0
        if index and index == len(chunks) - 1:
            first, second = range(2, n_row, 2), range(3, n_row, 2)
            *held[here], mark = weight_update(
                projector, shape, marks, far[0::2], held[here], part=(0, 0.5), masks=first, final=False
            )
            marks, far, masks, late = [mark], far[0::2] + far[1::2], [*first, *second], len(first)
        new, *_, mark = weight_update(
            projector, shape, marks, far, held[here], at,
            part=(0, 0.5), masks=masks, late=late, carried=new_weight,
        )
        new_weight, marks = [new], [mark]
    return (new_weight[0], *moments)


def solution(mesh):
    n_row, n_col = mesh.shape["row"], mesh.shape["col"]
    in_specs = (
        P("col", "row"),
        P("row", "col"),
        P("row", None),
        P("row", "col"),
        P("row", "col"),
        P("row", "col"),
    )
    out_specs = (P("row", "col"), P("row", "col"), P("row", "col"))
    return jax.shard_map(
        functools.partial(body, n_row, n_col),
        mesh=mesh,
        in_specs=in_specs,
        out_specs=out_specs,
        check_vma=False,
    )
```
